128 devices in a mesh: cells: 4 (over y_lo, core), genes: 32 (over x, z, y_hi).
Axes of the slice: x: 4, y: 4 (y_hi: 2, y_lo: 2; y = y_hi * 2 + y_lo), z: 4, core: 2. Of those that a mesh axis runs over, the one named last changes fastest.
Arguments:
- expression: float32 [640, 65536], P('cells', 'genes'), may hold values from -6 to 6
- omega_diag: float32 [256, 256, 256], P('genes'), may hold values from -0.25 to 2, as said below
- omega_offd: float32 [256, 6, 256, 256], P('genes'), may hold values from -0.3 to 0.3
- omega_src: int32 [256, 6], replicated, may hold values from 0 to 31, all different within a row; in each aligned block of 8 rows (0 to 7, 8 to 15, ...) at most 2 rows name the same one
- omega_off: int32 [256, 6], replicated, may hold values from 0 to 6
Outputs:
- new_diag: float32 [256, 256, 256], P(('genes', 'cells'))
- new_offd: float32 [256, 6, 256, 256], P(('genes', 'cells'))
The draws below stay inside these ranges and needn't reach their ends.
Inputs may be any that keep to these rules, and one draw needn't show every extreme that they name: `omega_src`: the 6 values of one row are distinct. Among the 8 rows of one index of genes (rows i * 8 to (i+1) * 8 - 1) no value appears more than 2 times, and in every draw some such group of rows names some value exactly 2 times. `omega_diag`: diagonal entries lie in 0.5 to 2; all other entries lie in -0.25 to 0.25.
All inputs are finite; a program needn't handle non-finite values.
Results may differ from the reference program's by a relative error of at most 0.000075.
Values sent between devices are 32-bit elements; how exact they have to be, the bound alone decides.
No kernel may reach another device: no remote copies, remote signals or barrier semaphores. Data moves between devices by JAX's collectives and lax.ppermute only.
A program may use at most 192 MiB of HBM per device.

```python
import math
import jax
import jax.numpy as jnp
import numpy as np
from jax import lax

BS = 256
K = 6
BLOCKS_DEV = 8
NBLK = 256
GENES = 65536
CELLS = 640
MOST = 2
N_GENES = 32


def draw_omega_diag(key, part):
    first, second = jax.random.split(jax.random.fold_in(key, 17))
    spread = jnp.clip(0.05 * jax.random.normal(first, (NBLK, BS, BS), jnp.float32), -0.25, 0.25)
    entries = jax.random.uniform(second, (NBLK, BS), jnp.float32, 0.5, 2.0)
    eye = jnp.eye(BS, dtype=jnp.float32)
    return spread * (1.0 - eye) + entries[:, :, None] * eye


def touch_ends(values, own_key, least, largest):
    longest = values.shape.index(max(values.shape))
    spots = []
    for shift in (0, 1):
        where = [jax.random.randint(jax.random.fold_in(own_key, axis), (), 0, length) for axis, length in enumerate(values.shape)]
        where[longest] = (where[longest] + shift) % values.shape[longest]
        spots.append(tuple(where))
    return values.at[spots[0]].set(least).at[spots[1]].set(largest)


def levels(rng, extent, cuts, smallest, high):
    gain, own = 1.0, jax.random.fold_in(rng, 6)
    for position, parts in cuts:
        heights = jnp.exp(jax.random.uniform(jax.random.fold_in(own, position), (parts,), jnp.float32, smallest / len(cuts), high / len(cuts)))
        gain = gain * jnp.repeat(heights, extent[position] // parts).reshape([-1 if axis == position else 1 for axis in range(len(extent))])
    return gain


def shared_out(rng, own, number, rows, number_of, top, reach, slope):
    sequence = jax.random.permutation(rng, number_of)
    crowded, usual = load_shares(number_of, rows * top, reach, slope, True), load_shares(number_of, rows * top, reach, slope, False)
    places = jnp.arange(number_of)

    def named(tallies, rotation):
        used = int((tallies > 0).sum())
        fixed = max(1, used // 4)
        shifted = fixed + (places - fixed + rotation * (used - fixed)) % max(1, number_of - fixed)
        return jnp.zeros((number_of,), jnp.int32).at[sequence[jnp.where(places < fixed, places, shifted)]].set(jnp.asarray(tallies, jnp.int32))

    tallies = jnp.where(number % 4 == 0, named(crowded, number // 4), named(usual, number - number // 4 - 1))
    mixed = jax.random.permutation(jax.random.fold_in(own, 3), number_of)
    donor, sink = mixed[0:number_of // 2 * 2:2], mixed[1:number_of // 2 * 2:2]
    slack = jnp.minimum(tallies[donor] - 1, reach - tallies[sink]) // 2
    slack = jnp.where((donor == sequence[0]) | (sink == sequence[0]) | (tallies[sink] == 0), 0, jnp.maximum(slack, 0))
    shifted = jax.random.randint(jax.random.fold_in(own, 4), (number_of // 2,), 0, 1 << 20) % (slack + 1)
    tallies = tallies.at[donor].add(-shifted).at[sink].add(shifted)
    members = jnp.searchsorted(jnp.cumsum(tallies), jnp.arange(rows * top), side="right").astype(jnp.int32)
    table = members.reshape(top, rows).T
    table = table[jax.random.permutation(jax.random.fold_in(own, 1), rows)]
    rotation = jax.random.randint(jax.random.fold_in(own, 2), (rows, 1), 0, top)
    return jnp.take_along_axis(table, (jnp.arange(top)[None, :] + rotation) % top, axis=1)


def load_shares(count, total, most, skew, full):
    loads = [(1 << 20) // math.isqrt(grade ** skew) + 1 for grade in range(1, count + 1)]
    largest = most if full else min(most, max(-(-total // count), total * loads[0] // sum(loads)))
    least = 1 if total - largest >= count - 1 else 0
    counts, spare = [largest] + [least] * (count - 1), total - largest - least * (count - 1)
    while spare > 0:
        free = [i for i in range(1, count) if counts[i] < largest] or [i for i in range(1, count) if counts[i] < most]
        whole, remaining = sum([loads[i] for i in free]), spare
        for i in free:
            more = min(most - counts[i], max(1, remaining * loads[i] // whole), spare)
            counts[i] = counts[i] + more
            spare = spare - more
    return np.array(counts)


def gaussian(stream_key, dims, width, most, cuts=(), kind=jnp.bfloat16):
    level = levels(stream_key, dims, cuts, -0.22, 0.18) if cuts else 1.0
    values = jax.random.normal(stream_key, dims, jnp.float32) * width * level
    return jnp.minimum(jnp.maximum(values, -most), most).astype(kind)


def setup_inputs(seed: int = 0) -> dict:
    arg_keys = jax.random.split(jax.random.key(seed), 6)
    expression = gaussian(arg_keys[0], (CELLS, GENES), 1.0, 6.0, ((0, 4), (1, 32)), jnp.float32)
    omega_diag = draw_omega_diag(jax.random.fold_in(arg_keys[5], 71), 0)
    omega_offd = gaussian(arg_keys[2], (NBLK, K, BS, BS), 0.05, 0.3, ((0, 32),), jnp.float32)
    omega_src_keys = jax.random.split(jax.random.fold_in(arg_keys[3], 1), NBLK // BLOCKS_DEV)
    omega_src_turns = jax.random.permutation(jax.random.fold_in(arg_keys[3], 3), NBLK // BLOCKS_DEV)
    omega_src = jax.vmap(lambda own, number: shared_out(jax.random.fold_in(arg_keys[3], 2), own, number, BLOCKS_DEV, N_GENES, K, MOST, 2))(omega_src_keys, omega_src_turns).reshape((NBLK, K))
    omega_off = touch_ends(jax.random.randint(arg_keys[4], (NBLK, K), 0, BLOCKS_DEV - 1), jax.random.fold_in(arg_keys[4], 1), 0, (BLOCKS_DEV - 1) - 1).astype(jnp.int32)
    return {"expression": expression, "omega_diag": omega_diag, "omega_offd": omega_offd, "omega_src": omega_src, "omega_off": omega_off}


def stored_rows(omega_src, omega_off, per_dev):
    cols = lax.broadcasted_iota(jnp.int32, omega_src.shape, 0)
    bump = jnp.logical_and(omega_src == cols // per_dev, omega_off >= cols % per_dev).astype(jnp.int32)
    return omega_src * per_dev + omega_off + bump


def shrink(values, limit):
    return values - jnp.clip(values, -limit, limit)


def reference(expression, omega_diag, omega_offd, omega_src, omega_off):
    highest = lax.Precision.HIGHEST
    cell_count = expression.shape[0]
    rows = stored_rows(omega_src, omega_off, BLOCKS_DEV)
    blocks = expression.reshape(cell_count, NBLK, BS)

    def column(j):
        own = lax.dynamic_index_in_dim(blocks, j, 1, keepdims=False)
        far = jnp.take(blocks, rows[j], axis=1)
        first = jnp.dot(own, omega_diag[j], precision=highest, preferred_element_type=omega_diag.dtype)
        return first + jnp.einsum('ckb,kbe->ce', far, omega_offd[j], precision=highest)

    outputs = lax.map(column, jnp.arange(NBLK, dtype=jnp.int32))

    def gradient(j):
        own_x = lax.dynamic_index_in_dim(blocks, j, 1, keepdims=False)
        own_y = outputs[j]
        far_x = jnp.take(blocks, rows[j], axis=1)
        far_y = jnp.take(outputs, rows[j], axis=0)
        diag_part = jnp.einsum('cb,ce->be', own_x, own_y, precision=highest)
        diag_part = diag_part + diag_part.T
        off_part = jnp.einsum('ckb,ce->kbe', far_x, own_y, precision=highest)
        off_part = off_part + jnp.einsum('kcb,ce->kbe', far_y, own_x, precision=highest)
        return diag_part, off_part

    diag_sum, off_sum = lax.map(gradient, jnp.arange(NBLK, dtype=jnp.int32))
    step_size = 0.5
    limit = step_size * 0.04
    scale = 1.0 / (2.0 * cell_count)
    eye = (lax.broadcasted_iota(jnp.int32, (BS, BS), 0) == lax.broadcasted_iota(jnp.int32, (BS, BS), 1)).astype(omega_diag.dtype)
    entries = jnp.sum(omega_diag * eye, axis=2)
    grad_diag = diag_sum * scale - eye * (1.0 / entries)[:, :, None]
    moved = omega_diag - step_size * grad_diag
    new_diag = eye * moved + (1.0 - eye) * shrink(moved, limit)
    new_offd = shrink(omega_offd - step_size * (off_sum * scale), limit)
    return new_diag, new_offd
```

```python
import functools

import jax
import jax.numpy as jnp
from jax import lax
from jax.experimental import pallas as pl
from jax.experimental.pallas import tpu as pltpu
from jax.sharding import PartitionSpec as P

PLANE = 16
MOST = 2
SIZES = (64, 64, 32)
X_ORDER = (2, 0, 1)
Y_ORDER = (0, 1, 2)
STEP = 0.5
LIMIT = STEP * 0.04


def halves(values):
    high = values.astype(jnp.bfloat16)
    low = (values - high.astype(jnp.float32)).astype(jnp.bfloat16)
    return high, low


def dot(left, right):
    return jnp.dot(left, right, preferred_element_type=jnp.float32)


def shrink(values):
    return values - jnp.clip(values, -LIMIT, LIMIT)


def pack_kernel(index, own, other, out, sem):
    n, slots = own.shape[0], out.shape[0] * out.shape[1]
    width = out.shape[3]

    @pl.loop(0, slots)
    def _(i):
        b = index[i]
        cols = pl.ds(pl.multiple_of((b % 8) * width, width), width)
        to = out.at[i // 4, i % 4]

        @pl.when(b < 8)
        def _():
            pltpu.make_async_copy(own.at[:, cols], to, sem).start()

        @pl.when(b >= 8)
        def _():
            pltpu.make_async_copy(other.at[:, cols], to, sem).start()

    pltpu.make_async_copy(out, out, sem).wait()


def pack(index, own, other):
    n, width = own.shape[0], 256
    return pl.pallas_call(
        pack_kernel,
        out_shape=jax.ShapeDtypeStruct((PLANE, 4, n, width), jnp.float32),
        in_specs=[
            pl.BlockSpec(memory_space=pltpu.SMEM),
            pl.BlockSpec(memory_space=pltpu.VMEM),
            pl.BlockSpec(memory_space=pltpu.VMEM),
        ],
        out_specs=pl.BlockSpec(memory_space=pl.ANY),
        scratch_shapes=[pltpu.SemaphoreType.DMA],
        compiler_params=pltpu.CompilerParams(vmem_limit_bytes=8 << 20),
        cost_estimate=pl.CostEstimate(
            flops=0, bytes_accessed=PLANE * 4 * n * width * 4, transcendentals=0
        ),
    )(index, own, other)


def share_kernel(pick, came, own, *refs):
    outs, sem = refs[:4], refs[4]
    width = came.shape[2]
    me = pick[48]
    for flip in range(4):
        place = me ^ flip

        @pl.loop(0, 2)
        def _(jj):
            col = place * 2 + jj
            for k in range(6):
                pltpu.make_async_copy(
                    came.at[pick[col * 6 + k]], outs[flip].at[jj * 7 + k], sem
                ).start()
            cols = pl.ds(pl.multiple_of(col * width, width), width)
            pltpu.make_async_copy(own.at[:, cols], outs[flip].at[jj * 7 + 6], sem).start()

    for flip in range(4):
        pltpu.make_async_copy(outs[flip], outs[flip], sem).wait()


def share(pick, came, own):
    n, width = own.shape[0], 256
    part = jax.ShapeDtypeStruct((14, n, width), jnp.float32)
    parts = pl.pallas_call(
        share_kernel,
        out_shape=[part] * 4,
        in_specs=[
            pl.BlockSpec(memory_space=pltpu.SMEM),
            pl.BlockSpec(memory_space=pl.ANY),
            pl.BlockSpec(memory_space=pl.ANY),
        ],
        out_specs=[pl.BlockSpec(memory_space=pl.ANY)] * 4,
        scratch_shapes=[pltpu.SemaphoreType.DMA],
        cost_estimate=pl.CostEstimate(
            flops=0, bytes_accessed=2 * 56 * n * width * 4, transcendentals=0
        ),
    )(pick, came, own)
    flipped = [
        lax.ppermute(parts[flip], "cells", [(c, c ^ flip) for c in range(4)])
        for flip in (2, 3, 1)
    ]
    return [parts[0]] + flipped


def product_kernel(pick, own, f0, f1, f2, f3, f4, f5, diag, offd, out):
    n = own.shape[0]
    total = jnp.zeros(out.shape, jnp.float32)
    for k, far in enumerate((f0, f1, f2, f3, f4, f5, None)):
        block = own[...] if far is None else far[0]
        weight = diag[0] if far is None else offd[0, k]
        high, low = halves(block)
        w_high, w_low = halves(weight)
        both = dot(jnp.concatenate([high, low], axis=0), w_high)
        total += both[:n] + both[n:] + dot(high, w_low)
    out[...] = total


def product(pick, own, came, diag, offd):
    n, width = own.shape[0], 256

    def far(k):
        return pl.BlockSpec((1, n, width), lambda j, pick: (pick[j * 6 + k], 0, 0))

    return pl.pallas_call(
        product_kernel,
        out_shape=jax.ShapeDtypeStruct(own.shape, jnp.float32),
        grid_spec=pltpu.PrefetchScalarGridSpec(
            num_scalar_prefetch=1,
            grid=(8,),
            in_specs=[pl.BlockSpec((n, width), lambda j, pick: (0, j))]
            + [far(k) for k in range(6)]
            + [
                pl.BlockSpec((1, width, width), lambda j, pick: (j, 0, 0)),
                pl.BlockSpec((1, 6, width, width), lambda j, pick: (j, 0, 0, 0)),
            ],
            out_specs=pl.BlockSpec((n, width), lambda j, pick: (0, j)),
        ),
        compiler_params=pltpu.CompilerParams(vmem_limit_bytes=24 << 20),
        cost_estimate=pl.CostEstimate(
            flops=2 * 3 * 56 * n * width * width,
            bytes_accessed=56 * width * width * 4 + 64 * n * width * 4,
            transcendentals=0,
        ),
    )(pick, own, came, came, came, came, came, came, diag, offd)


def step_kernel(parts, me, *refs):
    far_x, far_y = refs[:parts], refs[parts : 2 * parts]
    own_x, own_y = refs[2 * parts : 3 * parts], refs[3 * parts : 4 * parts]
    diag, offd, new_diag, new_offd, left_high, left_low = refs[4 * parts :]
    k = pl.program_id(1)
    scale = 1.0 / (2.0 * 640)
    width = 256

    @pl.when(k == 0)
    def _():
        at = 0
        for group in (own_y, own_x):
            for ref in group:
                high, low = halves(ref[0].T)
                n = ref.shape[1]
                left_high[:, at : at + n] = high
                left_low[:, at : at + n] = low
                at += n

    @pl.when(k < 6)
    def _():
        right = jnp.concatenate([ref[0] for ref in far_x + far_y], axis=0)
        high, low = halves(right)
        total = dot(left_high[...], high) + dot(left_low[...], high) + dot(left_high[...], low)
        new_offd[0, 0] = shrink(offd[0, 0] - (STEP * scale) * total.T)

    @pl.when(k == 6)
    def _():
        cells = left_high.shape[1] // 2
        right = jnp.concatenate([ref[0] for ref in own_x], axis=0)
        high, low = halves(right)
        y_high, y_low = left_high[:, :cells], left_low[:, :cells]
        total = dot(y_high, high) + dot(y_low, high) + dot(y_high, low)
        total = total + total.T
        eye = lax.broadcasted_iota(jnp.int32, (width, width), 0) == lax.broadcasted_iota(
            jnp.int32, (width, width), 1
        )
        old = diag[0]
        moved = old - STEP * (total * scale - jnp.where(eye, 1.0 / old, 0.0))
        new_diag[0] = jnp.where(eye, moved, shrink(moved))


def step(me, xs, ys, diag, offd):
    width, parts = 256, len(xs)

    def far(a):
        return pl.BlockSpec((1, a.shape[1], width), lambda j, k, me: (j * 7 + jnp.minimum(k, 5), 0, 0))

    def own(a):
        return pl.BlockSpec((1, a.shape[1], width), lambda j, k, me: (j * 7 + 6, 0, 0))

    return pl.pallas_call(
        functools.partial(step_kernel, parts),
        out_shape=[
            jax.ShapeDtypeStruct((2, width, width), jnp.float32),
            jax.ShapeDtypeStruct((2, 6, width, width), jnp.float32),
        ],
        grid_spec=pltpu.PrefetchScalarGridSpec(
            num_scalar_prefetch=1,
            grid=(2, 7),
            in_specs=[far(a) for a in xs]
            + [far(a) for a in ys]
            + [own(a) for a in xs]
            + [own(a) for a in ys]
            + [
                pl.BlockSpec((1, width, width), lambda j, k, me: (me[0] * 2 + j, 0, 0)),
                pl.BlockSpec(
                    (1, 1, width, width),
                    lambda j, k, me: (me[0] * 2 + j, jnp.minimum(k, 5), 0, 0),
                ),
            ],
            out_specs=[
                pl.BlockSpec((1, width, width), lambda j, k, me: (j, 0, 0)),
                pl.BlockSpec((1, 1, width, width), lambda j, k, me: (j, jnp.minimum(k, 5), 0, 0)),
            ],
            scratch_shapes=[
                pltpu.VMEM((width, 1280), jnp.bfloat16),
                pltpu.VMEM((width, 1280), jnp.bfloat16),
            ],
        ),
        compiler_params=pltpu.CompilerParams(vmem_limit_bytes=40 << 20),
        cost_estimate=pl.CostEstimate(
            flops=2 * 3 * 26 * 640 * width * width,
            bytes_accessed=28 * 640 * width * 4 + 28 * width * width * 4,
            transcendentals=0,
        ),
    )(me, *xs, *ys, *xs, *ys, diag, offd)


def tables(omega_src, omega_off):
    here = lax.axis_index("genes")
    cols = lax.broadcasted_iota(jnp.int32, omega_src.shape, 0)
    bump = jnp.logical_and(omega_src == cols // 8, omega_off >= cols % 8).astype(jnp.int32)
    block = (omega_off + bump).reshape(32, 48)
    src = omega_src.reshape(32, 48)
    earlier = lax.broadcasted_iota(jnp.int32, (48, 48), 0) > lax.broadcasted_iota(
        jnp.int32, (48, 48), 1
    )
    same = jnp.logical_and(src[:, :, None] == src[:, None, :], earlier[None])
    rank = jnp.sum(same.astype(jnp.int32), axis=2)
    y_hi = here % 2
    to_src = lax.dynamic_index_in_dim(src.reshape(PLANE, 2, 48), y_hi, 1, keepdims=False)
    to_rank = lax.dynamic_index_in_dim(rank.reshape(PLANE, 2, 48), y_hi, 1, keepdims=False)
    to_block = lax.dynamic_index_in_dim(block.reshape(PLANE, 2, 48), y_hi, 1, keepdims=False)
    slot = lax.broadcasted_iota(jnp.int32, (1, 4, 1), 1)
    source = (here // 2) * 2 + slot // 2
    match = jnp.logical_and(to_src[:, None, :] == source, to_rank[:, None, :] == slot % 2)
    send = jnp.sum(match.astype(jnp.int32) * to_block[:, None, :], axis=2)
    send = send + jnp.where(slot[:, :, 0] // 2 == y_hi, 0, 8)
    mine = lax.dynamic_index_in_dim(src, here, 0, keepdims=False)
    mine_rank = lax.dynamic_index_in_dim(rank, here, 0, keepdims=False)
    return send.reshape(-1), mine * MOST + mine_rank


def per_device(expression, omega_diag, omega_offd, omega_src, omega_off):
    me = lax.axis_index("cells").astype(jnp.int32)
    send, pick = tables(omega_src, omega_off)
    pick = jnp.concatenate([pick, me[None]])
    swap = [(g, g ^ 1) for g in range(32)]
    planes = [[p * 2 + y for p in range(PLANE)] for y in range(2)]

    def exchange(own):
        other = lax.ppermute(own, "genes", swap)
        sent = pack(send, own, other)
        came = lax.all_to_all(sent, "genes", 0, 0, axis_index_groups=planes)
        return came.reshape(PLANE * 4, own.shape[0], 256)

    starts = [sum(SIZES[:i]) for i in range(len(SIZES))]
    own_x = {i: lax.slice_in_dim(expression, starts[i], starts[i] + SIZES[i], axis=0) for i in X_ORDER}
    came_x = {i: exchange(own_x[i]) for i in X_ORDER}
    own_y = {i: product(pick, own_x[i], came_x[i], omega_diag, omega_offd) for i in X_ORDER}
    came_y = {i: exchange(own_y[i]) for i in Y_ORDER}
    xs, ys = [], []
    for i in Y_ORDER:
        xs += share(pick, came_x[i], own_x[i])
        ys += share(pick, came_y[i], own_y[i])
    return tuple(step(me[None], xs, ys, omega_diag, omega_offd))


def solution(mesh):
    return jax.shard_map(
        per_device,
        mesh=mesh,
        in_specs=(
            P("cells", "genes"),
            P("genes", None, None),
            P("genes", None, None, None),
            P(),
            P(),
        ),
        out_specs=(P(("genes", "cells"), None, None), P(("genes", "cells"), None, None, None)),
        check_vma=False,
    )
```

```python
import functools

import jax
import jax.numpy as jnp
from jax import lax
from jax.experimental import pallas as pl
from jax.experimental.pallas import tpu as pltpu
from jax.sharding import PartitionSpec as P

PLANE = 16
MOST = 2
SIZES = (48, 40, 40, 32)
LATE = 2
FLIPS = (0, 2, 3, 1)
STEP = 0.5
LIMIT = STEP * 0.04


def halves(values):
    high = values.astype(jnp.bfloat16)
    low = (values - high.astype(jnp.float32)).astype(jnp.bfloat16)
    return high, low


def dot(left, right):
    return jnp.dot(left, right, preferred_element_type=jnp.float32)


def shrink(values):
    return values - jnp.clip(values, -LIMIT, LIMIT)


def pack_kernel(index, own, other, *refs):
    out, sem = refs[-2:]
    slots, width = out.shape[0] * out.shape[1], out.shape[3]

    @pl.loop(0, slots)
    def _(i):
        b = index[i]
        cols = pl.ds(pl.multiple_of((b % 8) * width, width), width)
        to = out.at[i // 4, i % 4]

        @pl.when(b < 8)
        def _():
            pltpu.make_async_copy(own.at[:, cols], to, sem).start()

        @pl.when(b >= 8)
        def _():
            pltpu.make_async_copy(other.at[:, cols], to, sem).start()

    pltpu.make_async_copy(out, out, sem).wait()


def pack(index, own, other, before=()):
    n, width = own.shape[0], 256
    return pl.pallas_call(
        pack_kernel,
        out_shape=pltpu.HBM((PLANE, 4, n, width), jnp.float32),
        in_specs=[
            pl.BlockSpec(memory_space=pltpu.SMEM),
            pl.BlockSpec(memory_space=pltpu.VMEM),
            pl.BlockSpec(memory_space=pltpu.VMEM),
        ]
        + [pl.BlockSpec(memory_space=pl.ANY)] * len(before),
        out_specs=pl.BlockSpec(memory_space=pltpu.HBM),
        scratch_shapes=[pltpu.SemaphoreType.DMA],
        compiler_params=pltpu.CompilerParams(vmem_limit_bytes=8 << 20),
        cost_estimate=pl.CostEstimate(
            flops=0, bytes_accessed=PLANE * 4 * n * width * 4, transcendentals=0
        ),
    )(index, own, other, *before)


def share_kernel(pick, came, *refs):
    outs, held, sem_in, sem_out = refs[-7:-3], refs[-3], refs[-2], refs[-1]
    width, each = came.shape[2], held.shape[1] // 2
    me = pick[48]
    for flip in (2, 3, 1, 0):
        place = me ^ flip

        @pl.loop(0, 2)
        def _(jj):
            col = place * 2 + jj
            for k in range(6):
                pltpu.make_async_copy(
                    came.at[pick[col * 6 + k]], held.at[flip, jj * each + k], sem_in.at[flip]
                ).start()
            if each == 7:
                cols = pl.ds(pl.multiple_of(col * width, width), width)
                pltpu.make_async_copy(
                    refs[0].at[:, cols], held.at[flip, jj * each + 6], sem_in.at[flip]
                ).start()

    for flip in (2, 3, 1, 0):
        pltpu.make_async_copy(outs[flip], held.at[flip], sem_in.at[flip]).wait()
        pltpu.make_async_copy(held.at[flip], outs[flip], sem_out.at[flip]).start()
    for flip in (2, 3, 1, 0):
        pltpu.make_async_copy(held.at[flip], outs[flip], sem_out.at[flip]).wait()


def share(pick, came, own=(), before=()):
    n, width = came.shape[1:]
    blocks = 12 + 2 * len(own)
    part = pltpu.HBM((blocks, n, width), jnp.float32)
    return pl.pallas_call(
        share_kernel,
        out_shape=[part] * 4,
        in_specs=[pl.BlockSpec(memory_space=pltpu.SMEM), pl.BlockSpec(memory_space=pl.ANY)]
        + [pl.BlockSpec(memory_space=pl.ANY)] * (len(own) + len(before)),
        out_specs=[pl.BlockSpec(memory_space=pltpu.HBM)] * 4,
        scratch_shapes=[
            pltpu.VMEM((4, blocks, n, width), jnp.float32),
            pltpu.SemaphoreType.DMA((4,)),
            pltpu.SemaphoreType.DMA((4,)),
        ],
        compiler_params=pltpu.CompilerParams(vmem_limit_bytes=12 << 20),
        cost_estimate=pl.CostEstimate(
            flops=0, bytes_accessed=8 * blocks * n * width * 4, transcendentals=0
        ),
    )(pick, came, *own, *before)


def handed(parts):
    return [
        lax.ppermute(parts[flip], "cells", [(c, c ^ flip) for c in range(4)]) if flip else parts[0]
        for flip in FLIPS
    ]


def product_kernel(pick, own, f0, f1, f2, f3, f4, f5, diag, offd, out):
    n = own.shape[0]
    total = jnp.zeros(out.shape, jnp.float32)
    for k, far in enumerate((f0, f1, f2, f3, f4, f5, None)):
        block = own[...] if far is None else far[0]
        weight = diag[0] if far is None else offd[0, k]
        high, low = halves(block)
        w_high, w_low = halves(weight)
        both = dot(jnp.concatenate([high, low], axis=0), w_high)
        total += both[:n] + both[n:] + dot(high, w_low)
    out[...] = total


def product(pick, own, came, diag, offd):
    n, width = own.shape[0], 256

    def far(k):
        return pl.BlockSpec((1, n, width), lambda j, pick: (pick[j * 6 + k], 0, 0))

    return pl.pallas_call(
        product_kernel,
        out_shape=jax.ShapeDtypeStruct(own.shape, jnp.float32),
        grid_spec=pltpu.PrefetchScalarGridSpec(
            num_scalar_prefetch=1,
            grid=(8,),
            in_specs=[pl.BlockSpec((n, width), lambda j, pick: (0, j))]
            + [far(k) for k in range(6)]
            + [
                pl.BlockSpec((1, width, width), lambda j, pick: (j, 0, 0)),
                pl.BlockSpec((1, 6, width, width), lambda j, pick: (j, 0, 0, 0)),
            ],
            out_specs=pl.BlockSpec((n, width), lambda j, pick: (0, j)),
        ),
        compiler_params=pltpu.CompilerParams(vmem_limit_bytes=56 << 20),
        cost_estimate=pl.CostEstimate(
            flops=2 * 3 * 56 * n * width * width,
            bytes_accessed=56 * width * width * 4 + 64 * n * width * 4,
            transcendentals=0,
        ),
    )(pick, own, came, came, came, came, came, came, diag, offd)


def gram_kernel(starts, last, me, *refs):
    parts = 4 * len(starts)
    far_x, ys, home = refs[:parts], refs[parts : 2 * parts], refs[2 * parts : 2 * parts + 4]
    if last:
        diag_sum, off_sum, diag, offd = refs[2 * parts + 4 : 2 * parts + 8]
    new_diag, new_offd, left_high, left_low = refs[-4:]
    cells = left_high.shape[1] // 2
    scale = 1.0 / (2.0 * 640)
    width = 256
    own_x = [
        ref[starts[i] : starts[i] + far_x[4 * i].shape[1], :]
        for i in range(len(starts))
        for ref in home
    ]
    own_x = jnp.concatenate(own_x, axis=0)
    own_y = jnp.concatenate([ref[6] for ref in ys], axis=0)
    for at, value in ((0, own_y), (cells, own_x)):
        high, low = halves(value.T)
        left_high[:, at : at + cells] = high
        left_low[:, at : at + cells] = low
    for k in range(6):
        right = jnp.concatenate([ref[k] for ref in far_x + ys], axis=0)
        high, low = halves(right)
        total = dot(left_high[...], high) + dot(left_low[...], high) + dot(left_high[...], low)
        total = total.T
        if last:
            total = shrink(offd[0, k] - (STEP * scale) * (total + off_sum[0, k]))
        new_offd[0, k] = total
    high, low = halves(own_x)
    y_high, y_low = left_high[:, :cells], left_low[:, :cells]
    total = dot(y_high, high) + dot(y_low, high) + dot(y_high, low)
    if last:
        total = total + diag_sum[0]
        total = total + total.T
        eye = lax.broadcasted_iota(jnp.int32, (width, width), 0) == lax.broadcasted_iota(
            jnp.int32, (width, width), 1
        )
        old = diag[0]
        moved = old - STEP * (total * scale - jnp.where(eye, 1.0 / old, 0.0))
        total = jnp.where(eye, moved, shrink(moved))
    new_diag[0] = total


def gram(me, starts, xs, ys, home, sums=(), old=()):
    width = 256
    cells = sum(a.shape[1] for a in xs)

    def block(a):
        return pl.BlockSpec((a.shape[0] // 2, a.shape[1], width), lambda j, me: (j, 0, 0))

    def pair(base):
        return [
            pl.BlockSpec((1, width, width), lambda j, me: (base(me) + j, 0, 0)),
            pl.BlockSpec((1, 6, width, width), lambda j, me: (base(me) + j, 0, 0, 0)),
        ]

    specs = [block(a) for a in [*xs, *ys]]
    specs += [pl.BlockSpec((a.shape[0], width), lambda j, me: (0, j)) for a in home]
    if sums:
        specs += pair(lambda me: 0) + pair(lambda me: me[0] * 2)
    return pl.pallas_call(
        functools.partial(gram_kernel, starts, bool(sums)),
        out_shape=[
            jax.ShapeDtypeStruct((2, width, width), jnp.float32),
            jax.ShapeDtypeStruct((2, 6, width, width), jnp.float32),
        ],
        grid_spec=pltpu.PrefetchScalarGridSpec(
            num_scalar_prefetch=1,
            grid=(2,),
            in_specs=specs,
            out_specs=pair(lambda me: 0),
            scratch_shapes=[pltpu.VMEM((width, 2 * cells), jnp.bfloat16)] * 2,
        ),
        compiler_params=pltpu.CompilerParams(vmem_limit_bytes=56 << 20),
        cost_estimate=pl.CostEstimate(
            flops=2 * 3 * 26 * cells * width * width,
            bytes_accessed=28 * cells * width * 4 + 28 * width * width * 4,
            transcendentals=0,
        ),
    )(me, *xs, *ys, *home, *sums, *old)


def tables(omega_src, omega_off):
    here = lax.axis_index("genes")
    cols = lax.broadcasted_iota(jnp.int32, omega_src.shape, 0)
    bump = jnp.logical_and(omega_src == cols // 8, omega_off >= cols % 8).astype(jnp.int32)
    block = (omega_off + bump).reshape(32, 48)
    src = omega_src.reshape(32, 48)
    earlier = lax.broadcasted_iota(jnp.int32, (48, 48), 0) > lax.broadcasted_iota(
        jnp.int32, (48, 48), 1
    )
    same = jnp.logical_and(src[:, :, None] == src[:, None, :], earlier[None])
    rank = jnp.sum(same.astype(jnp.int32), axis=2)
    y_hi = here % 2
    to_src = lax.dynamic_index_in_dim(src.reshape(PLANE, 2, 48), y_hi, 1, keepdims=False)
    to_rank = lax.dynamic_index_in_dim(rank.reshape(PLANE, 2, 48), y_hi, 1, keepdims=False)
    to_block = lax.dynamic_index_in_dim(block.reshape(PLANE, 2, 48), y_hi, 1, keepdims=False)
    slot = lax.broadcasted_iota(jnp.int32, (1, 4, 1), 1)
    source = (here // 2) * 2 + slot // 2
    match = jnp.logical_and(to_src[:, None, :] == source, to_rank[:, None, :] == slot % 2)
    send = jnp.sum(match.astype(jnp.int32) * to_block[:, None, :], axis=2)
    send = send + jnp.where(slot[:, :, 0] // 2 == y_hi, 0, 8)
    mine = lax.dynamic_index_in_dim(src, here, 0, keepdims=False)
    mine_rank = lax.dynamic_index_in_dim(rank, here, 0, keepdims=False)
    return send.reshape(-1), mine * MOST + mine_rank


def per_device(expression, omega_diag, omega_offd, omega_src, omega_off):
    me = lax.axis_index("cells").astype(jnp.int32)
    send, pick = tables(omega_src, omega_off)
    pick = jnp.concatenate([pick, me[None]])
    swap = [(g, g ^ 1) for g in range(32)]
    planes = [[p * 2 + y for p in range(PLANE)] for y in range(2)]

    def exchange(sent):
        came = lax.all_to_all(sent, "genes", 0, 0, axis_index_groups=planes)
        return came.reshape(PLANE * 4, sent.shape[2], 256)

    runs = range(len(SIZES))
    starts = tuple(sum(SIZES[:i]) for i in runs)
    turns = [("x", i) for i in runs] + [("y", i) for i in runs]
    own, other, shared, parts = {}, {}, {}, {}
    slices = [lax.slice_in_dim(expression, starts[i], starts[i] + SIZES[i], axis=0) for i in runs]
    own["x", 0] = slices[0]
    other["x", 0] = lax.ppermute(slices[0], "genes", swap)
    sent = pack(send, own["x", 0], other["x", 0])
    sent, expression, *slices[1:] = lax.optimization_barrier((sent, expression, *slices[1:]))
    for i in runs[1:]:
        own["x", i] = slices[i]
        other["x", i] = lax.ppermute(slices[i], "genes", swap)
    home = handed(
        [lax.dynamic_slice_in_dim(expression, (me ^ flip) * 512, 512, axis=1) for flip in range(4)]
    )

    def summed(which, *rest):
        xs, ys = ([part for i in which for part in parts[kind, i]] for kind in "xy")
        return gram(me[None], tuple(starts[i] for i in which), xs, ys, home, *rest)

    for at, turn in enumerate(turns):
        kind, i = turn
        arrived = exchange(sent)
        if at + 1 < len(turns):
            then = turns[at + 1]
            if at == 0:
                before, ties = [other["x", j] for j in runs[2:]], home[1:]
            else:
                last = turns[at - 1]
                before, ties = [shared[last][0]], [parts[last][1], parts[last][3]]
                if last[0] == "x":
                    before.append(own["y", last[1]])
            if at >= 2:
                ties.append(parts[turns[at - 2]][2])
            if at >= 1 and last[0] == "x":
                ties.append(other["y", last[1]])
            sent = pack(send, own[then], other[then], before)
            sent, arrived, *ties = lax.optimization_barrier((sent, arrived, *ties))
            if at == 0:
                home[1:] = ties
            else:
                parts[last][1], parts[last][3] = ties[:2]
            if at >= 2:
                parts[turns[at - 2]][2] = ties[2]
            if at >= 1 and last[0] == "x":
                other["y", last[1]] = ties[-1]
        if kind == "x":
            shared[turn] = share(pick, arrived)
            own["y", i] = product(pick, own[turn], arrived, omega_diag, omega_offd)
            other["y", i] = lax.ppermute(own["y", i], "genes", swap)
        else:
            before = []
            if at + 1 == len(turns):
                sums = summed(runs[:-LATE])
                before = [sums[0]]
                last = turns[at - 1]
                arrived, *parts[last] = lax.optimization_barrier((arrived, *parts[last]))
            shared[turn] = share(pick, arrived, [own[turn]], before)
        parts[turn] = handed(shared[turn])
    return tuple(summed(runs[-LATE:], sums, (omega_diag, omega_offd)))


def solution(mesh):
    return jax.shard_map(
        per_device,
        mesh=mesh,
        in_specs=(
            P("cells", "genes"),
            P("genes", None, None),
            P("genes", None, None, None),
            P(),
            P(),
        ),
        out_specs=(P(("genes", "cells"), None, None), P(("genes", "cells"), None, None, None)),
        check_vma=False,
    )
```

```python
import functools

import jax
import jax.numpy as jnp
from jax import lax
from jax.experimental import pallas as pl
from jax.experimental.pallas import tpu as pltpu
from jax.sharding import PartitionSpec as P

PLANE = 16
MOST = 2
SIZES = (48, 40, 40, 32)
LATE = 2
SWAPPED = (0, 0, 0, 0)
FLIPS = (0, 2, 3, 1)
STEP = 0.5
LIMIT = STEP * 0.04


def halves(values):
    high = values.astype(jnp.bfloat16)
    low = (values - high.astype(jnp.float32)).astype(jnp.bfloat16)
    return high, low


def dot(left, right):
    return jnp.dot(left, right, preferred_element_type=jnp.float32)


def shrink(values):
    return values - jnp.clip(values, -LIMIT, LIMIT)


def pack_kernel(index, own, other, *refs):
    out, sem = refs[-2:]
    slots, width = out.shape[0] * out.shape[1], out.shape[3]

    @pl.loop(0, slots)
    def _(i):
        b = index[i]
        cols = pl.ds(pl.multiple_of((b % 8) * width, width), width)
        to = out.at[i // 4, i % 4]

        @pl.when(b < 8)
        def _():
            pltpu.make_async_copy(own.at[:, cols], to, sem).start()

        @pl.when(b >= 8)
        def _():
            pltpu.make_async_copy(other.at[:, cols], to, sem).start()

    pltpu.make_async_copy(out, out, sem).wait()


def pack(index, own, other, before=()):
    n, width = own.shape[0], 256
    return pl.pallas_call(
        pack_kernel,
        out_shape=pltpu.HBM((PLANE, 4, n, width), jnp.float32),
        in_specs=[
            pl.BlockSpec(memory_space=pltpu.SMEM),
            pl.BlockSpec(memory_space=pltpu.VMEM),
            pl.BlockSpec(memory_space=pltpu.VMEM),
        ]
        + [pl.BlockSpec(memory_space=pl.ANY)] * len(before),
        out_specs=pl.BlockSpec(memory_space=pltpu.HBM),
        scratch_shapes=[pltpu.SemaphoreType.DMA],
        compiler_params=pltpu.CompilerParams(vmem_limit_bytes=8 << 20),
        cost_estimate=pl.CostEstimate(
            flops=0, bytes_accessed=PLANE * 4 * n * width * 4, transcendentals=0
        ),
    )(index, own, other, *before)


def share_kernel(pick, came, *refs):
    outs, held, sem_in, sem_out = refs[-7:-3], refs[-3], refs[-2], refs[-1]
    width, each = came.shape[2], held.shape[1] // 2
    me = pick[48]
    for flip in (2, 3, 1, 0):
        place = me ^ flip

        @pl.loop(0, 2)
        def _(jj):
            col = place * 2 + jj
            for k in range(6):
                pltpu.make_async_copy(
                    came.at[pick[col * 6 + k]], held.at[flip, jj * each + k], sem_in.at[flip]
                ).start()
            if each == 7:
                cols = pl.ds(pl.multiple_of(col * width, width), width)
                pltpu.make_async_copy(
                    refs[0].at[:, cols], held.at[flip, jj * each + 6], sem_in.at[flip]
                ).start()

    for flip in (2, 3, 1, 0):
        pltpu.make_async_copy(outs[flip], held.at[flip], sem_in.at[flip]).wait()
        pltpu.make_async_copy(held.at[flip], outs[flip], sem_out.at[flip]).start()
    for flip in (2, 3, 1, 0):
        pltpu.make_async_copy(held.at[flip], outs[flip], sem_out.at[flip]).wait()


def share(pick, came, own=(), before=()):
    n, width = came.shape[1:]
    blocks = 12 + 2 * len(own)
    part = pltpu.HBM((blocks, n, width), jnp.float32)
    return pl.pallas_call(
        share_kernel,
        out_shape=[part] * 4,
        in_specs=[pl.BlockSpec(memory_space=pltpu.SMEM), pl.BlockSpec(memory_space=pl.ANY)]
        + [pl.BlockSpec(memory_space=pl.ANY)] * (len(own) + len(before)),
        out_specs=[pl.BlockSpec(memory_space=pltpu.HBM)] * 4,
        scratch_shapes=[
            pltpu.VMEM((4, blocks, n, width), jnp.float32),
            pltpu.SemaphoreType.DMA((4,)),
            pltpu.SemaphoreType.DMA((4,)),
        ],
        compiler_params=pltpu.CompilerParams(vmem_limit_bytes=12 << 20),
        cost_estimate=pl.CostEstimate(
            flops=0, bytes_accessed=8 * blocks * n * width * 4, transcendentals=0
        ),
    )(pick, came, *own, *before)


def handed(part, flip):
    return lax.ppermute(part, "cells", [(c, c ^ flip) for c in range(4)])


def product_kernel(pick, own, f0, f1, f2, f3, f4, f5, diag, offd, out):
    n = own.shape[0]
    total = jnp.zeros(out.shape, jnp.float32)
    for k, far in enumerate((f0, f1, f2, f3, f4, f5, None)):
        block = own[...] if far is None else far[0]
        weight = diag[0] if far is None else offd[0, k]
        high, low = halves(block)
        w_high, w_low = halves(weight)
        both = dot(jnp.concatenate([high, low], axis=0), w_high)
        total += both[:n] + both[n:] + dot(high, w_low)
    out[...] = total


def product(pick, own, came, diag, offd):
    n, width = own.shape[0], 256

    def far(k):
        return pl.BlockSpec((1, n, width), lambda j, pick: (pick[j * 6 + k], 0, 0))

    return pl.pallas_call(
        product_kernel,
        out_shape=jax.ShapeDtypeStruct(own.shape, jnp.float32),
        grid_spec=pltpu.PrefetchScalarGridSpec(
            num_scalar_prefetch=1,
            grid=(8,),
            in_specs=[pl.BlockSpec((n, width), lambda j, pick: (0, j))]
            + [far(k) for k in range(6)]
            + [
                pl.BlockSpec((1, width, width), lambda j, pick: (j, 0, 0)),
                pl.BlockSpec((1, 6, width, width), lambda j, pick: (j, 0, 0, 0)),
            ],
            out_specs=pl.BlockSpec((n, width), lambda j, pick: (0, j)),
        ),
        compiler_params=pltpu.CompilerParams(vmem_limit_bytes=56 << 20),
        cost_estimate=pl.CostEstimate(
            flops=2 * 3 * 56 * n * width * width,
            bytes_accessed=56 * width * width * 4 + 64 * n * width * 4,
            transcendentals=0,
        ),
    )(pick, own, came, came, came, came, came, came, diag, offd)


def gram_kernel(starts, more, last, me, *refs):
    parts = 4 * len(starts)
    far_x, ys, home = refs[:parts], refs[parts : 2 * parts], refs[2 * parts : 2 * parts + 4]
    if more:
        diag_sum, off_sum = refs[2 * parts + 4 : 2 * parts + 6]
    if last:
        diag, offd = refs[2 * parts + 6 : 2 * parts + 8]
    new_diag, new_offd, left_high, left_low = refs[-4:]
    cells = left_high.shape[1] // 2
    scale = 1.0 / (2.0 * 640)
    width = 256
    own_x = [
        ref[starts[i] : starts[i] + far_x[4 * i].shape[1], :]
        for i in range(len(starts))
        for ref in home
    ]
    own_x = jnp.concatenate(own_x, axis=0)
    own_y = jnp.concatenate([ref[6] for ref in ys], axis=0)
    for at, value in ((0, own_y), (cells, own_x)):
        high, low = halves(value.T)
        left_high[:, at : at + cells] = high
        left_low[:, at : at + cells] = low
    for k in range(6):
        right = jnp.concatenate([ref[k] for ref in far_x + ys], axis=0)
        high, low = halves(right)
        total = dot(left_high[...], high) + dot(left_low[...], high) + dot(left_high[...], low)
        total = total.T
        if more:
            total = total + off_sum[0, k]
        if last:
            total = shrink(offd[0, k] - (STEP * scale) * total)
        new_offd[0, k] = total
    high, low = halves(own_x)
    y_high, y_low = left_high[:, :cells], left_low[:, :cells]
    total = dot(y_high, high) + dot(y_low, high) + dot(y_high, low)
    if more:
        total = total + diag_sum[0]
    if last:
        total = total + total.T
        eye = lax.broadcasted_iota(jnp.int32, (width, width), 0) == lax.broadcasted_iota(
            jnp.int32, (width, width), 1
        )
        old = diag[0]
        moved = old - STEP * (total * scale - jnp.where(eye, 1.0 / old, 0.0))
        total = jnp.where(eye, moved, shrink(moved))
    new_diag[0] = total


def gram(me, starts, xs, ys, home, sums=(), old=()):
    width = 256
    cells = sum(a.shape[1] for a in xs)

    def block(a):
        return pl.BlockSpec((a.shape[0] // 2, a.shape[1], width), lambda j, me: (j, 0, 0))

    def pair(base):
        return [
            pl.BlockSpec((1, width, width), lambda j, me: (base(me) + j, 0, 0)),
            pl.BlockSpec((1, 6, width, width), lambda j, me: (base(me) + j, 0, 0, 0)),
        ]

    specs = [block(a) for a in [*xs, *ys]]
    specs += [pl.BlockSpec((a.shape[0], width), lambda j, me: (0, j)) for a in home]
    if sums:
        specs += pair(lambda me: 0)
    if old:
        specs += pair(lambda me: me[0] * 2)
    return pl.pallas_call(
        functools.partial(gram_kernel, starts, bool(sums), bool(old)),
        out_shape=[
            jax.ShapeDtypeStruct((2, width, width), jnp.float32),
            jax.ShapeDtypeStruct((2, 6, width, width), jnp.float32),
        ],
        grid_spec=pltpu.PrefetchScalarGridSpec(
            num_scalar_prefetch=1,
            grid=(2,),
            in_specs=specs,
            out_specs=pair(lambda me: 0),
            scratch_shapes=[pltpu.VMEM((width, 2 * cells), jnp.bfloat16)] * 2,
        ),
        compiler_params=pltpu.CompilerParams(vmem_limit_bytes=56 << 20),
        cost_estimate=pl.CostEstimate(
            flops=2 * 3 * 26 * cells * width * width,
            bytes_accessed=28 * cells * width * 4 + 28 * width * width * 4,
            transcendentals=0,
        ),
    )(me, *xs, *ys, *home, *sums, *old)


def tables(omega_src, omega_off):
    here = lax.axis_index("genes")
    cols = lax.broadcasted_iota(jnp.int32, omega_src.shape, 0)
    bump = jnp.logical_and(omega_src == cols // 8, omega_off >= cols % 8).astype(jnp.int32)
    block = (omega_off + bump).reshape(32, 48)
    src = omega_src.reshape(32, 48)
    earlier = lax.broadcasted_iota(jnp.int32, (48, 48), 0) > lax.broadcasted_iota(
        jnp.int32, (48, 48), 1
    )
    same = jnp.logical_and(src[:, :, None] == src[:, None, :], earlier[None])
    rank = jnp.sum(same.astype(jnp.int32), axis=2)
    y_hi = here % 2
    to_src = lax.dynamic_index_in_dim(src.reshape(PLANE, 2, 48), y_hi, 1, keepdims=False)
    to_rank = lax.dynamic_index_in_dim(rank.reshape(PLANE, 2, 48), y_hi, 1, keepdims=False)
    to_block = lax.dynamic_index_in_dim(block.reshape(PLANE, 2, 48), y_hi, 1, keepdims=False)
    slot = lax.broadcasted_iota(jnp.int32, (1, 4, 1), 1)
    source = (here // 2) * 2 + slot // 2
    match = jnp.logical_and(to_src[:, None, :] == source, to_rank[:, None, :] == slot % 2)
    send = jnp.sum(match.astype(jnp.int32) * to_block[:, None, :], axis=2)
    send = send + jnp.where(slot[:, :, 0] // 2 == y_hi, 0, 8)
    mine = lax.dynamic_index_in_dim(src, here, 0, keepdims=False)
    mine_rank = lax.dynamic_index_in_dim(rank, here, 0, keepdims=False)
    return send.reshape(-1), mine * MOST + mine_rank


def per_device(expression, omega_diag, omega_offd, omega_src, omega_off):
    me = lax.axis_index("cells").astype(jnp.int32)
    send, pick = tables(omega_src, omega_off)
    pick = jnp.concatenate([pick, me[None]])
    swap = [(g, g ^ 1) for g in range(32)]
    planes = [[p * 2 + y for p in range(PLANE)] for y in range(2)]

    def exchange(sent):
        came = lax.all_to_all(sent, "genes", 0, 0, axis_index_groups=planes)
        return came.reshape(PLANE * 4, sent.shape[2], 256)

    runs = range(len(SIZES))
    starts = tuple(sum(SIZES[:i]) for i in runs)
    turns = [("x", i) for i in runs] + [("y", i) for i in runs]
    own, other, shared, parts = {}, {}, {}, {}
    slices = [lax.slice_in_dim(expression, starts[i], starts[i] + SIZES[i], axis=0) for i in runs]
    own["x", 0] = slices[0]
    other["x", 0] = lax.ppermute(slices[0], "genes", swap)
    sent = pack(send, own["x", 0], other["x", 0])
    sent, expression, *slices[1:] = lax.optimization_barrier((sent, expression, *slices[1:]))
    for i in runs[1:]:
        own["x", i] = slices[i]
        other["x", i] = lax.ppermute(slices[i], "genes", swap)
    home = [
        lax.dynamic_slice_in_dim(expression, (me ^ flip) * 512, 512, axis=1) for flip in FLIPS
    ]
    home[1:] = [handed(piece, flip) for piece, flip in zip(home[1:], FLIPS[1:])]

    def summed(which, *rest):
        xs, ys = ([part for i in which for part in parts[kind, i]] for kind in "xy")
        return gram(me[None], tuple(starts[i] for i in which), xs, ys, home, *rest)

    for at, turn in enumerate(turns):
        kind, i = turn
        arrived = exchange(sent)
        if at + 1 < len(turns):
            then, before, ties = turns[at + 1], [], [arrived]
            if at == 0:
                before = [other["x", j] for j in runs[2:]]
                ties += home[1:]
            else:
                last = turns[at - 1]
                before = [shared[last][0]]
                ties += [shared[last][3], parts[last][1], parts[last][3]]
                if last[0] == "x":
                    before.append(own["y", last[1]])
                if at >= 2:
                    ties.append(parts[turns[at - 2]][2])
                due = [j for j in runs if j + 1 + SWAPPED[j] == at]
                ties += [other["y", j] for j in due]
            sent = pack(send, own[then], other[then], before)
            sent, arrived, *ties = lax.optimization_barrier((sent, *ties))
            if at == 0:
                home[1:] = ties
            else:
                for j in reversed(due):
                    other["y", j] = ties.pop()
                if at >= 2:
                    parts[turns[at - 2]][2] = ties.pop()
                parts[last][2] = handed(ties[0], 3)
                parts[last][1], parts[last][3] = ties[1:]
        before = []
        if at + 1 == len(turns):
            last = turns[at - 1]
            parts[last][2] = handed(shared[last][3], 3)
            sums = summed(runs[:-LATE])
            before = [sums[0]]
        if kind == "x":
            shared[turn] = share(pick, arrived)
            own["y", i] = product(pick, own[turn], arrived, omega_diag, omega_offd)
            other["y", i] = lax.ppermute(own["y", i], "genes", swap)
        else:
            shared[turn] = share(pick, arrived, [own[turn]], before)
        parts[turn] = [shared[turn][0], handed(shared[turn][2], 2), None, handed(shared[turn][1], 1)]
    parts[turn][2] = handed(shared[turn][3], 3)
    for i in runs[-LATE:-1]:
        sums = summed([i], sums)
    return tuple(summed(runs[-1:], sums, (omega_diag, omega_offd)))


def solution(mesh):
    return jax.shard_map(
        per_device,
        mesh=mesh,
        in_specs=(
            P("cells", "genes"),
            P("genes", None, None),
            P("genes", None, None, None),
            P(),
            P(),
        ),
        out_specs=(P(("genes", "cells"), None, None), P(("genes", "cells"), None, None, None)),
        check_vma=False,
    )
```

```python
import functools

import jax
import jax.numpy as jnp
from jax import lax
from jax.experimental import pallas as pl
from jax.experimental.pallas import tpu as pltpu
from jax.sharding import PartitionSpec as P

PLANE = 16
MOST = 2
SIZES = (48, 40, 40, 32)
LATE = 2
ORDER = (3, 0, 1, 2)
HOME = 1
EARLY = 1
SWAPPED = (0, 0, 0, 0)
FLIPS = (0, 2, 3, 1)
STEP = 0.5
LIMIT = STEP * 0.04


def halves(values):
    high = values.astype(jnp.bfloat16)
    low = (values - high.astype(jnp.float32)).astype(jnp.bfloat16)
    return high, low


def dot(left, right):
    return jnp.dot(left, right, preferred_element_type=jnp.float32)


def shrink(values):
    return values - jnp.clip(values, -LIMIT, LIMIT)


def pack_kernel(index, own, other, *refs):
    out, sem = refs[-2:]
    slots, width = out.shape[0] * out.shape[1], out.shape[3]

    @pl.loop(0, slots)
    def _(i):
        b = index[i]
        cols = pl.ds(pl.multiple_of((b % 8) * width, width), width)
        to = out.at[i // 4, i % 4]

        @pl.when(b < 8)
        def _():
            pltpu.make_async_copy(own.at[:, cols], to, sem).start()

        @pl.when(b >= 8)
        def _():
            pltpu.make_async_copy(other.at[:, cols], to, sem).start()

    pltpu.make_async_copy(out, out, sem).wait()


def pack(index, own, other, before=()):
    n, width = own.shape[0], 256
    return pl.pallas_call(
        pack_kernel,
        out_shape=pltpu.HBM((PLANE, 4, n, width), jnp.float32),
        in_specs=[
            pl.BlockSpec(memory_space=pltpu.SMEM),
            pl.BlockSpec(memory_space=pltpu.VMEM),
            pl.BlockSpec(memory_space=pltpu.VMEM),
        ]
        + [pl.BlockSpec(memory_space=pl.ANY)] * len(before),
        out_specs=pl.BlockSpec(memory_space=pltpu.HBM),
        scratch_shapes=[pltpu.SemaphoreType.DMA],
        compiler_params=pltpu.CompilerParams(vmem_limit_bytes=8 << 20),
        cost_estimate=pl.CostEstimate(
            flops=0, bytes_accessed=PLANE * 4 * n * width * 4, transcendentals=0
        ),
    )(index, own, other, *before)


def share_kernel(pick, came, *refs):
    outs, held, sem_in, sem_out = refs[-7:-3], refs[-3], refs[-2], refs[-1]
    width, each = came.shape[2], held.shape[1] // 2
    me = pick[48]
    for flip in (2, 3, 1, 0):
        place = me ^ flip

        @pl.loop(0, 2)
        def _(jj):
            col = place * 2 + jj
            for k in range(6):
                pltpu.make_async_copy(
                    came.at[pick[col * 6 + k]], held.at[flip, jj * each + k], sem_in.at[flip]
                ).start()
            if each == 7:
                cols = pl.ds(pl.multiple_of(col * width, width), width)
                pltpu.make_async_copy(
                    refs[0].at[:, cols], held.at[flip, jj * each + 6], sem_in.at[flip]
                ).start()

    for flip in (2, 3, 1, 0):
        pltpu.make_async_copy(outs[flip], held.at[flip], sem_in.at[flip]).wait()
        pltpu.make_async_copy(held.at[flip], outs[flip], sem_out.at[flip]).start()
    for flip in (2, 3, 1, 0):
        pltpu.make_async_copy(held.at[flip], outs[flip], sem_out.at[flip]).wait()


def share(pick, came, own=(), before=()):
    n, width = came.shape[1:]
    blocks = 12 + 2 * len(own)
    part = pltpu.HBM((blocks, n, width), jnp.float32)
    return pl.pallas_call(
        share_kernel,
        out_shape=[part] * 4,
        in_specs=[pl.BlockSpec(memory_space=pltpu.SMEM), pl.BlockSpec(memory_space=pl.ANY)]
        + [pl.BlockSpec(memory_space=pl.ANY)] * (len(own) + len(before)),
        out_specs=[pl.BlockSpec(memory_space=pltpu.HBM)] * 4,
        scratch_shapes=[
            pltpu.VMEM((4, blocks, n, width), jnp.float32),
            pltpu.SemaphoreType.DMA((4,)),
            pltpu.SemaphoreType.DMA((4,)),
        ],
        compiler_params=pltpu.CompilerParams(vmem_limit_bytes=12 << 20),
        cost_estimate=pl.CostEstimate(
            flops=0, bytes_accessed=8 * blocks * n * width * 4, transcendentals=0
        ),
    )(pick, came, *own, *before)


def handed(part, flip):
    return lax.ppermute(part, "cells", [(c, c ^ flip) for c in range(4)])


def product_kernel(pick, own, f0, f1, f2, f3, f4, f5, diag, offd, out):
    n = own.shape[0]
    total = jnp.zeros(out.shape, jnp.float32)
    for k, far in enumerate((f0, f1, f2, f3, f4, f5, None)):
        block = own[...] if far is None else far[0]
        weight = diag[0] if far is None else offd[0, k]
        high, low = halves(block)
        w_high, w_low = halves(weight)
        both = dot(jnp.concatenate([high, low], axis=0), w_high)
        total += both[:n] + both[n:] + dot(high, w_low)
    out[...] = total


def product(pick, own, came, diag, offd):
    n, width = own.shape[0], 256

    def far(k):
        return pl.BlockSpec((1, n, width), lambda j, pick: (pick[j * 6 + k], 0, 0))

    return pl.pallas_call(
        product_kernel,
        out_shape=jax.ShapeDtypeStruct(own.shape, jnp.float32),
        grid_spec=pltpu.PrefetchScalarGridSpec(
            num_scalar_prefetch=1,
            grid=(8,),
            in_specs=[pl.BlockSpec((n, width), lambda j, pick: (0, j))]
            + [far(k) for k in range(6)]
            + [
                pl.BlockSpec((1, width, width), lambda j, pick: (j, 0, 0)),
                pl.BlockSpec((1, 6, width, width), lambda j, pick: (j, 0, 0, 0)),
            ],
            out_specs=pl.BlockSpec((n, width), lambda j, pick: (0, j)),
        ),
        compiler_params=pltpu.CompilerParams(vmem_limit_bytes=56 << 20),
        cost_estimate=pl.CostEstimate(
            flops=2 * 3 * 56 * n * width * width,
            bytes_accessed=56 * width * width * 4 + 64 * n * width * 4,
            transcendentals=0,
        ),
    )(pick, own, came, came, came, came, came, came, diag, offd)


def gram_kernel(starts, more, last, me, *refs):
    parts = 4 * len(starts)
    far_x, ys, home = refs[:parts], refs[parts : 2 * parts], refs[2 * parts : 2 * parts + 4]
    if more:
        diag_sum, off_sum = refs[2 * parts + 4 : 2 * parts + 6]
    if last:
        diag, offd = refs[2 * parts + 6 : 2 * parts + 8]
    new_diag, new_offd, left_high, left_low = refs[-4:]
    cells = left_high.shape[1] // 2
    scale = 1.0 / (2.0 * 640)
    width = 256
    own_x = [
        ref[starts[i] : starts[i] + far_x[4 * i].shape[1], :]
        for i in range(len(starts))
        for ref in home
    ]
    own_x = jnp.concatenate(own_x, axis=0)
    own_y = jnp.concatenate([ref[6] for ref in ys], axis=0)
    for at, value in ((0, own_y), (cells, own_x)):
        high, low = halves(value.T)
        left_high[:, at : at + cells] = high
        left_low[:, at : at + cells] = low
    for k in range(6):
        right = jnp.concatenate([ref[k] for ref in far_x + ys], axis=0)
        high, low = halves(right)
        total = dot(left_high[...], high) + dot(left_low[...], high) + dot(left_high[...], low)
        total = total.T
        if more:
            total = total + off_sum[0, k]
        if last:
            total = shrink(offd[0, k] - (STEP * scale) * total)
        new_offd[0, k] = total
    high, low = halves(own_x)
    y_high, y_low = left_high[:, :cells], left_low[:, :cells]
    total = dot(y_high, high) + dot(y_low, high) + dot(y_high, low)
    if more:
        total = total + diag_sum[0]
    if last:
        total = total + total.T
        eye = lax.broadcasted_iota(jnp.int32, (width, width), 0) == lax.broadcasted_iota(
            jnp.int32, (width, width), 1
        )
        old = diag[0]
        moved = old - STEP * (total * scale - jnp.where(eye, 1.0 / old, 0.0))
        total = jnp.where(eye, moved, shrink(moved))
    new_diag[0] = total


def gram(me, starts, xs, ys, home, sums=(), old=()):
    width = 256
    cells = sum(a.shape[1] for a in xs)

    def block(a):
        return pl.BlockSpec((a.shape[0] // 2, a.shape[1], width), lambda j, me: (j, 0, 0))

    def pair(base):
        return [
            pl.BlockSpec((1, width, width), lambda j, me: (base(me) + j, 0, 0)),
            pl.BlockSpec((1, 6, width, width), lambda j, me: (base(me) + j, 0, 0, 0)),
        ]

    specs = [block(a) for a in [*xs, *ys]]
    specs += [pl.BlockSpec((a.shape[0], width), lambda j, me: (0, j)) for a in home]
    if sums:
        specs += pair(lambda me: 0)
    if old:
        specs += pair(lambda me: me[0] * 2)
    return pl.pallas_call(
        functools.partial(gram_kernel, starts, bool(sums), bool(old)),
        out_shape=[
            jax.ShapeDtypeStruct((2, width, width), jnp.float32),
            jax.ShapeDtypeStruct((2, 6, width, width), jnp.float32),
        ],
        grid_spec=pltpu.PrefetchScalarGridSpec(
            num_scalar_prefetch=1,
            grid=(2,),
            in_specs=specs,
            out_specs=pair(lambda me: 0),
            scratch_shapes=[pltpu.VMEM((width, 2 * cells), jnp.bfloat16)] * 2,
        ),
        compiler_params=pltpu.CompilerParams(vmem_limit_bytes=56 << 20),
        cost_estimate=pl.CostEstimate(
            flops=2 * 3 * 26 * cells * width * width,
            bytes_accessed=28 * cells * width * 4 + 28 * width * width * 4,
            transcendentals=0,
        ),
    )(me, *xs, *ys, *home, *sums, *old)


def tables(omega_src, omega_off):
    here = lax.axis_index("genes")
    cols = lax.broadcasted_iota(jnp.int32, omega_src.shape, 0)
    bump = jnp.logical_and(omega_src == cols // 8, omega_off >= cols % 8).astype(jnp.int32)
    block = (omega_off + bump).reshape(32, 48)
    src = omega_src.reshape(32, 48)
    earlier = lax.broadcasted_iota(jnp.int32, (48, 48), 0) > lax.broadcasted_iota(
        jnp.int32, (48, 48), 1
    )
    same = jnp.logical_and(src[:, :, None] == src[:, None, :], earlier[None])
    rank = jnp.sum(same.astype(jnp.int32), axis=2)
    y_hi = here % 2
    to_src = lax.dynamic_index_in_dim(src.reshape(PLANE, 2, 48), y_hi, 1, keepdims=False)
    to_rank = lax.dynamic_index_in_dim(rank.reshape(PLANE, 2, 48), y_hi, 1, keepdims=False)
    to_block = lax.dynamic_index_in_dim(block.reshape(PLANE, 2, 48), y_hi, 1, keepdims=False)
    slot = lax.broadcasted_iota(jnp.int32, (1, 4, 1), 1)
    source = (here // 2) * 2 + slot // 2
    match = jnp.logical_and(to_src[:, None, :] == source, to_rank[:, None, :] == slot % 2)
    send = jnp.sum(match.astype(jnp.int32) * to_block[:, None, :], axis=2)
    send = send + jnp.where(slot[:, :, 0] // 2 == y_hi, 0, 8)
    mine = lax.dynamic_index_in_dim(src, here, 0, keepdims=False)
    mine_rank = lax.dynamic_index_in_dim(rank, here, 0, keepdims=False)
    return send.reshape(-1), mine * MOST + mine_rank


def per_device(expression, omega_diag, omega_offd, omega_src, omega_off):
    me = lax.axis_index("cells").astype(jnp.int32)
    send, pick = tables(omega_src, omega_off)
    pick = jnp.concatenate([pick, me[None]])
    swap = [(g, g ^ 1) for g in range(32)]
    planes = [[p * 2 + y for p in range(PLANE)] for y in range(2)]

    def exchange(sent):
        came = lax.all_to_all(sent, "genes", 0, 0, axis_index_groups=planes)
        return came.reshape(PLANE * 4, sent.shape[2], 256)

    runs = range(len(SIZES))
    starts = tuple(sum(SIZES[:i]) for i in runs)
    turns = [("x", i) for i in ORDER] + [("y", i) for i in runs]
    own, other, shared, parts = {}, {}, {}, {}
    slices = [lax.slice_in_dim(expression, starts[i], starts[i] + SIZES[i], axis=0) for i in runs]
    first = ORDER[0]
    own["x", first] = slices[first]
    other["x", first] = lax.ppermute(slices[first], "genes", swap)
    sent = pack(send, own["x", first], other["x", first])
    rest = [slices[i] for i in ORDER[1:]]
    sent, expression, *rest = lax.optimization_barrier((sent, expression, *rest))
    for i, piece in zip(ORDER[1:], rest):
        own["x", i] = piece
        other["x", i] = lax.ppermute(piece, "genes", swap)
    home = [
        lax.dynamic_slice_in_dim(expression, (me ^ flip) * 512, 512, axis=1) for flip in FLIPS
    ]
    home[1:] = [handed(piece, flip) for piece, flip in zip(home[1:], FLIPS[1:])]

    def summed(which, *rest):
        xs, ys = ([part for i in which for part in parts[kind, i]] for kind in "xy")
        return gram(me[None], tuple(starts[i] for i in which), xs, ys, home, *rest)

    for at, turn in enumerate(turns):
        kind, i = turn
        arrived = exchange(sent)
        if at + 1 < len(turns):
            then, before, ties = turns[at + 1], [], [arrived]
            if at == 0:
                before = [other["x", j] for j in ORDER[2 : 2 + EARLY]]
            else:
                last = turns[at - 1]
                before = [shared[last][0]]
                if at == 1:
                    before += [other["x", j] for j in ORDER[2 + EARLY :]]
                ties += [shared[last][3], parts[last][1], parts[last][3]]
                if last[0] == "x":
                    before.append(own["y", last[1]])
                if at >= 2:
                    ties.append(parts[turns[at - 2]][2])
                due = [j for j in runs if ORDER.index(j) + 1 + SWAPPED[j] == at]
                ties += [other["y", j] for j in due]
            if at == HOME:
                ties += home[1:]
            sent = pack(send, own[then], other[then], before)
            sent, arrived, *ties = lax.optimization_barrier((sent, *ties))
            if at == HOME:
                home[1:] = ties[-3:]
                ties = ties[:-3]
            if at:
                for j in reversed(due):
                    other["y", j] = ties.pop()
                if at >= 2:
                    parts[turns[at - 2]][2] = ties.pop()
                parts[last][2] = handed(ties[0], 3)
                parts[last][1], parts[last][3] = ties[1:]
        before = []
        if at + 1 == len(turns):
            last = turns[at - 1]
            parts[last][2] = handed(shared[last][3], 3)
            sums = summed(runs[:-LATE])
            before = [sums[0]]
        if kind == "x":
            shared[turn] = share(pick, arrived)
            own["y", i] = product(pick, own[turn], arrived, omega_diag, omega_offd)
            other["y", i] = lax.ppermute(own["y", i], "genes", swap)
        else:
            shared[turn] = share(pick, arrived, [own[turn]], before)
        parts[turn] = [shared[turn][0], handed(shared[turn][2], 2), None, handed(shared[turn][1], 1)]
    parts[turn][2] = handed(shared[turn][3], 3)
    for i in runs[-LATE:-1]:
        sums = summed([i], sums)
    return tuple(summed(runs[-1:], sums, (omega_diag, omega_offd)))


def solution(mesh):
    return jax.shard_map(
        per_device,
        mesh=mesh,
        in_specs=(
            P("cells", "genes"),
            P("genes", None, None),
            P("genes", None, None, None),
            P(),
            P(),
        ),
        out_specs=(P(("genes", "cells"), None, None), P(("genes", "cells"), None, None, None)),
        check_vma=False,
    )
```

```python
import functools

import jax
import jax.numpy as jnp
from jax import lax
from jax.experimental import pallas as pl
from jax.experimental.pallas import tpu as pltpu
from jax.sharding import PartitionSpec as P

PLANE = 16
MOST = 2
SIZES = (48, 40, 40, 32)
LATE = 2
ORDER = (3, 0, 1, 2)
HOME = 1
EARLY = 0
SWAPPED = (0, 0, 0, 0)
FLIPS = (0, 2, 3, 1)
STEP = 0.5
LIMIT = STEP * 0.04


def halves(values):
    high = values.astype(jnp.bfloat16)
    low = (values - high.astype(jnp.float32)).astype(jnp.bfloat16)
    return high, low


def dot(left, right):
    return jnp.dot(left, right, preferred_element_type=jnp.float32)


def shrink(values):
    return values - jnp.clip(values, -LIMIT, LIMIT)


def pack_kernel(index, own, other, *refs):
    out, sem = refs[-2:]
    slots, width = out.shape[0] * out.shape[1], out.shape[3]

    @pl.loop(0, slots)
    def _(i):
        b = index[i]
        cols = pl.ds(pl.multiple_of((b % 8) * width, width), width)
        to = out.at[i // 4, i % 4]

        @pl.when(b < 8)
        def _():
            pltpu.make_async_copy(own.at[:, cols], to, sem).start()

        @pl.when(b >= 8)
        def _():
            pltpu.make_async_copy(other.at[:, cols], to, sem).start()

    pltpu.make_async_copy(out, out, sem).wait()


def pack(index, own, other, before=()):
    n, width = own.shape[0], 256
    return pl.pallas_call(
        pack_kernel,
        out_shape=pltpu.HBM((PLANE, 4, n, width), jnp.float32),
        in_specs=[
            pl.BlockSpec(memory_space=pltpu.SMEM),
            pl.BlockSpec(memory_space=pltpu.VMEM),
            pl.BlockSpec(memory_space=pltpu.VMEM),
        ]
        + [pl.BlockSpec(memory_space=pl.ANY)] * len(before),
        out_specs=pl.BlockSpec(memory_space=pltpu.HBM),
        scratch_shapes=[pltpu.SemaphoreType.DMA],
        compiler_params=pltpu.CompilerParams(vmem_limit_bytes=8 << 20),
        cost_estimate=pl.CostEstimate(
            flops=0, bytes_accessed=PLANE * 4 * n * width * 4, transcendentals=0
        ),
    )(index, own, other, *before)


def share_kernel(pick, came, *refs):
    outs, held, sem_in, sem_out = refs[-7:-3], refs[-3], refs[-2], refs[-1]
    width, each = came.shape[2], held.shape[1] // 2
    me = pick[48]
    for flip in (2, 3, 1, 0):
        place = me ^ flip

        @pl.loop(0, 2)
        def _(jj):
            col = place * 2 + jj
            for k in range(6):
                pltpu.make_async_copy(
                    came.at[pick[col * 6 + k]], held.at[flip, jj * each + k], sem_in.at[flip]
                ).start()
            if each == 7:
                cols = pl.ds(pl.multiple_of(col * width, width), width)
                pltpu.make_async_copy(
                    refs[0].at[:, cols], held.at[flip, jj * each + 6], sem_in.at[flip]
                ).start()

    for flip in (2, 3, 1, 0):
        pltpu.make_async_copy(outs[flip], held.at[flip], sem_in.at[flip]).wait()
        pltpu.make_async_copy(held.at[flip], outs[flip], sem_out.at[flip]).start()
    for flip in (2, 3, 1, 0):
        pltpu.make_async_copy(held.at[flip], outs[flip], sem_out.at[flip]).wait()


def share(pick, came, own=(), before=()):
    n, width = came.shape[1:]
    blocks = 12 + 2 * len(own)
    part = pltpu.HBM((blocks, n, width), jnp.float32)
    return pl.pallas_call(
        share_kernel,
        out_shape=[part] * 4,
        in_specs=[pl.BlockSpec(memory_space=pltpu.SMEM), pl.BlockSpec(memory_space=pl.ANY)]
        + [pl.BlockSpec(memory_space=pl.ANY)] * (len(own) + len(before)),
        out_specs=[pl.BlockSpec(memory_space=pltpu.HBM)] * 4,
        scratch_shapes=[
            pltpu.VMEM((4, blocks, n, width), jnp.float32),
            pltpu.SemaphoreType.DMA((4,)),
            pltpu.SemaphoreType.DMA((4,)),
        ],
        compiler_params=pltpu.CompilerParams(vmem_limit_bytes=12 << 20),
        cost_estimate=pl.CostEstimate(
            flops=0, bytes_accessed=8 * blocks * n * width * 4, transcendentals=0
        ),
    )(pick, came, *own, *before)


def handed(part, flip):
    return lax.ppermute(part, "cells", [(c, c ^ flip) for c in range(4)])


def product_kernel(pick, own, f0, f1, f2, f3, f4, f5, diag, offd, out):
    n = own.shape[0]
    total = jnp.zeros(out.shape, jnp.float32)
    for k, far in enumerate((f0, f1, f2, f3, f4, f5, None)):
        block = own[...] if far is None else far[0]
        weight = diag[0] if far is None else offd[0, k]
        high, low = halves(block)
        w_high, w_low = halves(weight)
        both = dot(jnp.concatenate([high, low], axis=0), w_high)
        total += both[:n] + both[n:] + dot(high, w_low)
    out[...] = total


def product(pick, own, came, diag, offd):
    n, width = own.shape[0], 256

    def far(k):
        return pl.BlockSpec((1, n, width), lambda j, pick: (pick[j * 6 + k], 0, 0))

    return pl.pallas_call(
        product_kernel,
        out_shape=jax.ShapeDtypeStruct(own.shape, jnp.float32),
        grid_spec=pltpu.PrefetchScalarGridSpec(
            num_scalar_prefetch=1,
            grid=(8,),
            in_specs=[pl.BlockSpec((n, width), lambda j, pick: (0, j))]
            + [far(k) for k in range(6)]
            + [
                pl.BlockSpec((1, width, width), lambda j, pick: (j, 0, 0)),
                pl.BlockSpec((1, 6, width, width), lambda j, pick: (j, 0, 0, 0)),
            ],
            out_specs=pl.BlockSpec((n, width), lambda j, pick: (0, j)),
        ),
        compiler_params=pltpu.CompilerParams(vmem_limit_bytes=56 << 20),
        cost_estimate=pl.CostEstimate(
            flops=2 * 3 * 56 * n * width * width,
            bytes_accessed=56 * width * width * 4 + 64 * n * width * 4,
            transcendentals=0,
        ),
    )(pick, own, came, came, came, came, came, came, diag, offd)


def gram_kernel(starts, more, last, me, *refs):
    parts = 4 * len(starts)
    far_x, ys, home = refs[:parts], refs[parts : 2 * parts], refs[2 * parts : 2 * parts + 4]
    if more:
        diag_sum, off_sum = refs[2 * parts + 4 : 2 * parts + 6]
    if last:
        diag, offd = refs[2 * parts + 6 : 2 * parts + 8]
    new_diag, new_offd, left_high, left_low = refs[-4:]
    cells = left_high.shape[1] // 2
    scale = 1.0 / (2.0 * 640)
    width = 256
    own_x = [
        ref[starts[i] : starts[i] + far_x[4 * i].shape[1], :]
        for i in range(len(starts))
        for ref in home
    ]
    own_x = jnp.concatenate(own_x, axis=0)
    own_y = jnp.concatenate([ref[6] for ref in ys], axis=0)
    for at, value in ((0, own_y), (cells, own_x)):
        high, low = halves(value.T)
        left_high[:, at : at + cells] = high
        left_low[:, at : at + cells] = low
    for k in range(6):
        right = jnp.concatenate([ref[k] for ref in far_x + ys], axis=0)
        high, low = halves(right)
        total = dot(left_high[...], high) + dot(left_low[...], high) + dot(left_high[...], low)
        total = total.T
        if more:
            total = total + off_sum[0, k]
        if last:
            total = shrink(offd[0, k] - (STEP * scale) * total)
        new_offd[0, k] = total
    high, low = halves(own_x)
    y_high, y_low = left_high[:, :cells], left_low[:, :cells]
    total = dot(y_high, high) + dot(y_low, high) + dot(y_high, low)
    if more:
        total = total + diag_sum[0]
    if last:
        total = total + total.T
        eye = lax.broadcasted_iota(jnp.int32, (width, width), 0) == lax.broadcasted_iota(
            jnp.int32, (width, width), 1
        )
        old = diag[0]
        moved = old - STEP * (total * scale - jnp.where(eye, 1.0 / old, 0.0))
        total = jnp.where(eye, moved, shrink(moved))
    new_diag[0] = total


def gram(me, starts, xs, ys, home, sums=(), old=()):
    width = 256
    cells = sum(a.shape[1] for a in xs)

    def block(a):
        return pl.BlockSpec((a.shape[0] // 2, a.shape[1], width), lambda j, me: (j, 0, 0))

    def pair(base):
        return [
            pl.BlockSpec((1, width, width), lambda j, me: (base(me) + j, 0, 0)),
            pl.BlockSpec((1, 6, width, width), lambda j, me: (base(me) + j, 0, 0, 0)),
        ]

    specs = [block(a) for a in [*xs, *ys]]
    specs += [pl.BlockSpec((a.shape[0], width), lambda j, me: (0, j)) for a in home]
    if sums:
        specs += pair(lambda me: 0)
    if old:
        specs += pair(lambda me: me[0] * 2)
    return pl.pallas_call(
        functools.partial(gram_kernel, starts, bool(sums), bool(old)),
        out_shape=[
            jax.ShapeDtypeStruct((2, width, width), jnp.float32),
            jax.ShapeDtypeStruct((2, 6, width, width), jnp.float32),
        ],
        grid_spec=pltpu.PrefetchScalarGridSpec(
            num_scalar_prefetch=1,
            grid=(2,),
            in_specs=specs,
            out_specs=pair(lambda me: 0),
            scratch_shapes=[pltpu.VMEM((width, 2 * cells), jnp.bfloat16)] * 2,
        ),
        compiler_params=pltpu.CompilerParams(vmem_limit_bytes=56 << 20),
        cost_estimate=pl.CostEstimate(
            flops=2 * 3 * 26 * cells * width * width,
            bytes_accessed=28 * cells * width * 4 + 28 * width * width * 4,
            transcendentals=0,
        ),
    )(me, *xs, *ys, *home, *sums, *old)


def tables(omega_src, omega_off):
    here = lax.axis_index("genes")
    cols = lax.broadcasted_iota(jnp.int32, omega_src.shape, 0)
    bump = jnp.logical_and(omega_src == cols // 8, omega_off >= cols % 8).astype(jnp.int32)
    block = (omega_off + bump).reshape(32, 48)
    src = omega_src.reshape(32, 48)
    earlier = lax.broadcasted_iota(jnp.int32, (48, 48), 0) > lax.broadcasted_iota(
        jnp.int32, (48, 48), 1
    )
    same = jnp.logical_and(src[:, :, None] == src[:, None, :], earlier[None])
    rank = jnp.sum(same.astype(jnp.int32), axis=2)
    y_hi = here % 2
    to_src = lax.dynamic_index_in_dim(src.reshape(PLANE, 2, 48), y_hi, 1, keepdims=False)
    to_rank = lax.dynamic_index_in_dim(rank.reshape(PLANE, 2, 48), y_hi, 1, keepdims=False)
    to_block = lax.dynamic_index_in_dim(block.reshape(PLANE, 2, 48), y_hi, 1, keepdims=False)
    slot = lax.broadcasted_iota(jnp.int32, (1, 4, 1), 1)
    source = (here // 2) * 2 + slot // 2
    match = jnp.logical_and(to_src[:, None, :] == source, to_rank[:, None, :] == slot % 2)
    send = jnp.sum(match.astype(jnp.int32) * to_block[:, None, :], axis=2)
    send = send + jnp.where(slot[:, :, 0] // 2 == y_hi, 0, 8)
    mine = lax.dynamic_index_in_dim(src, here, 0, keepdims=False)
    mine_rank = lax.dynamic_index_in_dim(rank, here, 0, keepdims=False)
    return send.reshape(-1), mine * MOST + mine_rank


def per_device(expression, omega_diag, omega_offd, omega_src, omega_off):
    me = lax.axis_index("cells").astype(jnp.int32)
    send, pick = tables(omega_src, omega_off)
    pick = jnp.concatenate([pick, me[None]])
    swap = [(g, g ^ 1) for g in range(32)]
    planes = [[p * 2 + y for p in range(PLANE)] for y in range(2)]

    def exchange(sent):
        came = lax.all_to_all(sent, "genes", 0, 0, axis_index_groups=planes)
        return came.reshape(PLANE * 4, sent.shape[2], 256)

    runs = range(len(SIZES))
    starts = tuple(sum(SIZES[:i]) for i in runs)
    turns = [("x", i) for i in ORDER] + [("y", i) for i in runs]
    own, other, shared, parts = {}, {}, {}, {}
    slices = [lax.slice_in_dim(expression, starts[i], starts[i] + SIZES[i], axis=0) for i in runs]
    first = ORDER[0]
    own["x", first] = slices[first]
    other["x", first] = lax.ppermute(slices[first], "genes", swap)
    sent = pack(send, own["x", first], other["x", first])
    rest = [slices[i] for i in ORDER[1:]]
    sent, expression, *rest = lax.optimization_barrier((sent, expression, *rest))
    for i, piece in zip(ORDER[1:], rest):
        own["x", i] = piece
        other["x", i] = lax.ppermute(piece, "genes", swap)
    home = [
        lax.dynamic_slice_in_dim(expression, (me ^ flip) * 512, 512, axis=1) for flip in FLIPS
    ]
    home[1:] = [handed(piece, flip) for piece, flip in zip(home[1:], FLIPS[1:])]

    def summed(which, *rest):
        xs, ys = ([part for i in which for part in parts[kind, i]] for kind in "xy")
        return gram(me[None], tuple(starts[i] for i in which), xs, ys, home, *rest)

    for at, turn in enumerate(turns):
        kind, i = turn
        arrived = exchange(sent)
        if at + 1 < len(turns):
            then, before, ties = turns[at + 1], [], [arrived]
            if at == 0:
                before = [other["x", j] for j in ORDER[2 : 2 + EARLY]]
            else:
                last = turns[at - 1]
                before = [shared[last][0]]
                if at == 1:
                    before += [other["x", j] for j in ORDER[2 + EARLY :]]
                ties += [shared[last][3], parts[last][1], parts[last][3]]
                if last[0] == "x":
                    before.append(own["y", last[1]])
                if at >= 2:
                    ties.append(parts[turns[at - 2]][2])
                due = [j for j in runs if ORDER.index(j) + 1 + SWAPPED[j] == at]
                ties += [other["y", j] for j in due]
            if at == HOME:
                ties += home[1:]
            sent = pack(send, own[then], other[then], before)
            sent, arrived, *ties = lax.optimization_barrier((sent, *ties))
            if at == HOME:
                home[1:] = ties[-3:]
                ties = ties[:-3]
            if at:
                for j in reversed(due):
                    other["y", j] = ties.pop()
                if at >= 2:
                    parts[turns[at - 2]][2] = ties.pop()
                parts[last][2] = handed(ties[0], 3)
                parts[last][1], parts[last][3] = ties[1:]
        before = []
        if at + 1 == len(turns):
            last = turns[at - 1]
            parts[last][2] = handed(shared[last][3], 3)
            sums = summed(runs[:-LATE])
            before = [sums[0]]
        if kind == "x":
            shared[turn] = share(pick, arrived)
            own["y", i] = product(pick, own[turn], arrived, omega_diag, omega_offd)
            other["y", i] = lax.ppermute(own["y", i], "genes", swap)
        else:
            shared[turn] = share(pick, arrived, [own[turn]], before)
        parts[turn] = [shared[turn][0], handed(shared[turn][2], 2), None, handed(shared[turn][1], 1)]
    parts[turn][2] = handed(shared[turn][3], 3)
    for i in runs[-LATE:-1]:
        sums = summed([i], sums)
    return tuple(summed(runs[-1:], sums, (omega_diag, omega_offd)))


def solution(mesh):
    return jax.shard_map(
        per_device,
        mesh=mesh,
        in_specs=(
            P("cells", "genes"),
            P("genes", None, None),
            P("genes", None, None, None),
            P(),
            P(),
        ),
        out_specs=(P(("genes", "cells"), None, None), P(("genes", "cells"), None, None, None)),
        check_vma=False,
    )
```
